32 devices in a mesh: dp: 2 (over core), expert: 16 (over z, y, x).
Axes of the slice: x: 2, y: 2, z: 4, core: 2. Of those that a mesh axis runs over, the one named last changes fastest.
Arguments:
- tokens: bfloat16 [2048, 4096], P('expert', 'dp'), may hold values from -6 to 6
- gates: float32 [2048, 8], P('expert'), may hold values from 0.03 to 0.5
- expert_ids: int32 [2048, 8], P('expert'), may hold values from 0 to 15, as said below
- d_mixed: bfloat16 [2048, 4096], P('expert', 'dp'), may hold values from -6 to 6
- w_up: bfloat16 [16, 4096, 1024], P('expert', 'dp'), may hold values from -0.09375 to 0.09375
- w_down: bfloat16 [16, 1024, 4096], P('expert', None, 'dp'), may hold values from -0.1875 to 0.1875
Outputs:
- mixed: bfloat16 [2048, 4096], P('expert', 'dp')
- d_tokens: bfloat16 [2048, 4096], P('expert', 'dp')
- grad_up: bfloat16 [16, 4096, 1024], P('expert', 'dp')
- grad_down: bfloat16 [16, 1024, 4096], P('expert', None, 'dp')
The draws below stay inside these ranges and needn't reach their ends.
Inputs may be any that keep to these rules, and one draw needn't show every extreme that they name: `expert_ids`: each row names 8 different experts. In the tokens of one device (aligned blocks of 128 rows) one expert, the same for every device, is named by exactly 64 tokens, and every other expert by at most 64 tokens; both bounds are reached on every device.
All inputs are finite; a program needn't handle non-finite values.
Results may differ from the reference program's by a relative error of at most 0.025.
Values may be sent and summed in bfloat16 or wider, within the bound.
A program may use at most 128 MiB of HBM per device.

```python
import math
import jax
import jax.numpy as jnp
from jax import lax

D = 4096
FF = 1024
TOP_K = 8
TOK_DEV = 128
EXPERTS = 16
TOKENS = 2048
HOT = 64
N_DP = 2


def draw_expert_ids(key, part):
    key = jax.random.fold_in(key, 11)
    hot_expert = jax.random.randint(jax.random.fold_in(key, 1), (), 0, EXPERTS).astype(jnp.int32)
    block_count = TOKENS // TOK_DEV
    block_keys = jax.random.split(jax.random.fold_in(key, 2), block_count)

    def one_block(block_key):
        key_a, key_b, key_c = jax.random.split(block_key, 3)
        shuffle = jax.random.permutation(key_a, TOK_DEV)
        position = jnp.argsort(shuffle, stable=True)
        has_hot = (position < HOT).astype(jnp.int32)
        slot_pick = jax.random.randint(key_b, (TOK_DEV,), 0, TOP_K)
        shuffled = jax.random.permutation(key_c, EXPERTS).astype(jnp.int32)
        cold_list = shuffled[jnp.argsort((shuffled == hot_expert).astype(jnp.int32), stable=True)][:EXPERTS - 1]
        slot_ids = jnp.arange(TOP_K, dtype=jnp.int32)[None, :]
        is_hot = ((has_hot[:, None] == 1) & (slot_ids == slot_pick[:, None])).astype(jnp.int32)
        flat_hot = is_hot.reshape(TOK_DEV * TOP_K)
        cold_index = jnp.cumsum(1 - flat_hot) - (1 - flat_hot)
        cold_expert = cold_list[cold_index % (EXPERTS - 1)]
        return jnp.where(flat_hot == 1, hot_expert, cold_expert).reshape(TOK_DEV, TOP_K)
    return jax.vmap(one_block)(block_keys).reshape(TOKENS, TOP_K).astype(jnp.int32)


def shard_levels(own_key, shape, shards, smallest, high):
    def one(dim, shards_of):
        steps = jax.random.uniform(jax.random.fold_in(jax.random.fold_in(own_key, 6), dim), (shards_of,), jnp.float32, smallest / len(shards), high / len(shards))
        return jnp.repeat(jnp.exp(steps), shape[dim] // shards_of).reshape((-1,) + (1,) * (len(shape) - dim - 1))

    loudness = one(*shards[0])
    for cut in shards[1:]:
        loudness = loudness * one(*cut)
    return loudness


def bell_draw(rng, extent, scale, bound, shards=(), kind=jnp.bfloat16):
    gain = shard_levels(rng, extent, shards, -0.22, 0.18) if shards else 1.0
    result = jax.random.normal(rng, extent, jnp.float32) * scale * gain
    return jnp.minimum(jnp.maximum(result, -bound), bound).astype(kind)


def setup_inputs(seed: int = 0) -> dict:
    seeds = jax.random.split(jax.random.key(seed), 7)
    return {
        "tokens": bell_draw(seeds[0], (TOKENS, D), 1.0, 6.0, ((0, 16), (1, 2))),
        "gates": jnp.clip(jnp.exp(math.log(0.5) - 2.8134107 * jax.random.uniform(seeds[1], (TOKENS, TOP_K), jnp.float32) ** shard_levels(seeds[1], (TOKENS, TOP_K), ((0, 16),), -0.2, 0.2)), 0.03, 0.5),
        "expert_ids": draw_expert_ids(jax.random.fold_in(seeds[6], 71), 0),
        "d_mixed": bell_draw(seeds[3], (TOKENS, D), 0.5, 6.0, ((0, 16), (1, 2))),
        "w_up": bell_draw(seeds[4], (EXPERTS, D, FF), D ** -0.5, 0.09375, ((0, 16), (1, 2))),
        "w_down": bell_draw(seeds[5], (EXPERTS, FF, D), FF ** -0.5, 0.1875, ((0, 16), (2, 2))),
    }


def split_product(row_block, weight_blocks, pattern):
    partials = jnp.einsum(pattern, row_block.astype(jnp.float32), weight_blocks.astype(jnp.float32))
    partials = lax.optimization_barrier(partials.astype(jnp.bfloat16))
    return jnp.sum(partials.astype(jnp.float32), 0)


def reference(tokens, gates, expert_ids, d_mixed, w_up, w_down):
    pair_count = TOKENS * TOP_K
    part_width = D // N_DP
    routed = expert_ids.reshape(pair_count)
    onehot = (routed[:, None] == jnp.arange(EXPERTS, dtype=jnp.int32)[None, :]).astype(jnp.int32)
    counts = jnp.sum(onehot, 0)
    order_in = jnp.sum((jnp.cumsum(onehot, 0) - onehot) * onehot, 1)
    padded = (counts + 127) // 128 * 128
    offsets = jnp.cumsum(padded) - padded
    position = (offsets[routed] + order_in).astype(jnp.int32)
    blocks = (pair_count + 127) // 128 + EXPERTS
    source = jnp.full((blocks * 128,), pair_count, jnp.int32).at[position].set(jnp.arange(pair_count, dtype=jnp.int32))
    token_index = jnp.where(source < pair_count, source // TOP_K, TOKENS).astype(jnp.int32)
    zero_row = jnp.zeros((1, D), jnp.bfloat16)
    row_blocks = jnp.concatenate([tokens, zero_row], 0)[token_index].reshape(blocks, 128, D)
    scaled = (gates[:, :, None] * d_mixed[:, None, :].astype(jnp.float32)).astype(jnp.bfloat16).reshape(pair_count, D)
    scaled_blocks = jnp.concatenate([scaled, zero_row], 0)[source].reshape(blocks, 128, D)
    starts = jnp.arange(blocks, dtype=jnp.int32) * 128
    block_expert = jnp.minimum(jnp.sum((starts[:, None] >= (offsets + padded)[None, :]).astype(jnp.int32), 1), EXPERTS - 1).astype(jnp.int32)
    contract_rows = (((0,), (0,)), ((), ()))

    def block_step(totals, inputs):
        up_total, down_total = totals
        block_rows, block_scaled, expert = inputs
        up_weight = w_up[expert]
        down_weight = w_down[expert]
        pre_act = split_product(block_rows.reshape(128, N_DP, part_width), up_weight.reshape(N_DP, part_width, FF), "rjd,jdf->jrf")
        hidden = jax.nn.silu(pre_act).astype(jnp.bfloat16)
        expert_out = jnp.dot(hidden, down_weight, preferred_element_type=jnp.float32).astype(jnp.bfloat16)
        back_sum = split_product(block_scaled.reshape(128, N_DP, part_width), down_weight.reshape(FF, N_DP, part_width), "rjd,fjd->jrf")
        logistic = jax.nn.sigmoid(pre_act)
        grad_pre = (back_sum * logistic * (1.0 + pre_act * (1.0 - logistic))).astype(jnp.bfloat16)
        grad_in = lax.dot_general(grad_pre, up_weight, (((1,), (1,)), ((), ())), preferred_element_type=jnp.float32).astype(jnp.bfloat16)
        up_total = up_total.at[expert].add(lax.dot_general(block_rows, grad_pre, contract_rows, preferred_element_type=jnp.float32))
        down_total = down_total.at[expert].add(lax.dot_general(hidden, block_scaled, contract_rows, preferred_element_type=jnp.float32))
        return (up_total, down_total), (expert_out, grad_in)

    start_totals = (jnp.zeros((EXPERTS, D, FF), jnp.float32), jnp.zeros((EXPERTS, FF, D), jnp.float32))
    (up_total, down_total), (block_outs, block_ins) = lax.scan(block_step, start_totals, (row_blocks, scaled_blocks, block_expert))
    pair_out = block_outs.reshape(blocks * 128, D)[position].reshape(TOKENS, TOP_K, D)
    mixed = jnp.sum(gates[:, :, None] * pair_out.astype(jnp.float32), 1).astype(jnp.bfloat16)
    pair_in = block_ins.reshape(blocks * 128, D)[position].reshape(TOKENS, TOP_K, D)
    d_tokens = jnp.sum(pair_in.astype(jnp.float32), 1).astype(jnp.bfloat16)
    return mixed, d_tokens, up_total.astype(jnp.bfloat16), down_total.astype(jnp.bfloat16)
```

```python
import functools

import jax
import jax.numpy as jnp
from jax import lax
from jax.experimental import pallas as pl
from jax.experimental.pallas import tpu as pltpu
from jax.sharding import PartitionSpec as P

MESH = pl.DeviceIdType.MESH
F32 = jnp.float32
BF16 = jnp.bfloat16


def tiles(extent, size, body):
    size = min(size, extent)

    def step(j, carry):
        body(pl.multiple_of(j * size, size), size)
        return carry

    lax.fori_loop(0, extent // size, step, 0)


def flip(value, mask, limit):
    result = value
    bit = 1
    while bit < limit:
        on = (mask // bit) % 2
        result = result + bit * on * (1 - 2 * ((value // bit) % 2))
        bit *= 2
    return result


def mm(a, b, da, db):
    return lax.dot_general(a, b, (((da,), (db,)), ((), ())), preferred_element_type=F32)


def kernel(
    cfg,
    tok, gates, ids, dmix, w_up, w_down,
    mixed, dtok, grad_up, grad_down,
    gt, sx, rows, wu, wd, part, rsbuf, hid, pre, own, cx, cy, cz, mt, mx,
    zs, zr, mzs, mzr, ys, yr, mys, myr, xs, xr, mxs, mxr,
    rss, rsr, ags, agr, cxs, cxr, cys, cyr, czs, czr, loc,
):
    groups, nd, t_rows, top, feat, ff, cap = cfg
    planes = groups // 4
    count = 2 * planes
    half = 2 * cap
    chunk = 4 * cap
    share = chunk // nd
    e = lax.axis_index("expert")
    me = lax.axis_index("dp")
    z, y, x = e // 4, (e // 2) % 2, e % 2
    e_x = e + 1 - 2 * x
    e_y = e + 2 - 4 * y

    def ring_of(i):
        return (i + i // planes) % planes

    def z_peer(r):
        return flip(z, r, planes) * 4 + y * 2 + x

    def send(src, dst, ssem, rsem, expert=None, dp=None):
        where = {"expert": expert} if dp is None else {"dp": dp}
        return pltpu.make_async_remote_copy(
            src_ref=src, dst_ref=dst, send_sem=ssem, recv_sem=rsem,
            device_id=where, device_id_type=MESH,
        )

    def z_copy(i, src):
        return send(src, gt.at[i, 0], zs.at[i], zr.at[i], z_peer(ring_of(i)))

    def mz_copy(i):
        return send(mt.at[0, 0], mt.at[i, 0], mzs.at[i], mzr.at[i], z_peer(ring_of(i)))

    def y_copy(i):
        return send(gt.at[i, 0], gt.at[i, 1], ys.at[i], yr.at[i], e_y)

    def my_copy(i):
        return send(mt.at[i, 0], mt.at[i, 1], mys.at[i], myr.at[i], e_y)

    def x_copy(i, yy):
        return send(
            sx.at[i, pl.ds(yy * cap, cap)], rows.at[i, pl.ds(half + yy * cap, cap)],
            xs.at[i, yy], xr.at[i, yy], e_x,
        )

    def mx_copy(i, yy):
        return send(mt.at[i, yy], mx.at[i, yy], mxs.at[i, yy], mxr.at[i, yy], e_x)

    def rs_copy(i, o):
        peer = (me + o) % nd
        return send(
            part.at[i % 2, pl.ds(pl.multiple_of(peer * share, share), share)],
            rsbuf.at[i, o - 1], rss.at[i, o - 1], rsr.at[i, o - 1], dp=peer,
        )

    def ag_copy(i, o):
        mine = hid.at[i, pl.ds(pl.multiple_of(me * share, share), share)]
        return send(mine, mine, ags.at[i, o - 1], agr.at[i, o - 1], dp=(me + o) % nd)

    def cx_copy(i):
        return send(sx.at[i], cx.at[i], cxs.at[i], cxr.at[i], e_x)

    def cy_copy(i):
        return send(gt.at[i, 1], cy.at[i], cys.at[i], cyr.at[i], e_y)

    def cz_copy(i):
        return send(gt.at[i, 0], cz.at[i], czs.at[i], czr.at[i], z_peer(ring_of(i)))

    tok_in = pltpu.make_async_copy(tok, gt.at[0, 0], loc.at[0])
    dmix_in = pltpu.make_async_copy(dmix, gt.at[count - 1, 0], loc.at[1])
    wu_in = pltpu.make_async_copy(w_up.at[0], wu, loc.at[2])
    wd_in = pltpu.make_async_copy(w_down.at[0], wd, loc.at[3])
    tok_in.start()
    dmix_in.start()
    wu_in.start()
    wd_in.start()

    barrier = pltpu.get_barrier_semaphore()
    peers = [{"expert": z_peer(r)} for r in range(1, planes)]
    peers += [{"expert": e_x}, {"expert": e_y}]
    peers += [{"dp": (me + o) % nd} for o in range(1, nd)]
    for peer in peers:
        pl.semaphore_signal(barrier, inc=1, device_id=peer, device_id_type=MESH)
    pl.semaphore_wait(barrier, len(peers))

    for i in range(1, planes):
        z_copy(i, tok).start()

    lane = lax.broadcasted_iota(jnp.int32, (t_rows, t_rows), 1)
    row = lax.broadcasted_iota(jnp.int32, (t_rows, t_rows), 0)
    chosen = jnp.zeros((t_rows, t_rows), F32)
    weight = jnp.zeros((t_rows, t_rows), F32)
    for k in range(top):
        hit = ids[:, k : k + 1] == lane
        chosen = chosen + jnp.where(hit, 1.0, 0.0)
        weight = weight + jnp.where(hit, gates[:, k : k + 1], 0.0)
    before = jnp.where(lane < row, 1.0, 0.0).astype(BF16)
    place = mm(before, chosen.astype(BF16), 1, 0)
    place = jnp.where(chosen > 0.0, place, -1.0)
    mt[0, 0, :groups, :] = jnp.transpose(place)[:groups]
    mt[0, 0, groups:, :] = jnp.transpose(weight)[:groups]
    for i in range(1, planes):
        mz_copy(i).start()

    slot = lax.broadcasted_iota(jnp.int32, (cap, t_rows), 0).astype(F32)

    def pick(table, expert):
        hot = slot == table[pl.ds(expert, 1), :]
        gate = jnp.sum(jnp.where(hot, table[pl.ds(groups + expert, 1), :], 0.0), 1, keepdims=True)
        return jnp.where(hot, 1.0, 0.0).astype(BF16), gate

    def select(i, yy):
        r = ring_of(i)
        hot_n, gate_n = pick(mt.at[r, yy], e_x)
        hot_o, gate_o = pick(mt.at[r, yy], e)
        hot = jnp.concatenate([hot_n, hot_o], 0)
        gate = jnp.concatenate([gate_n, gate_o], 0)
        gate = jnp.where(i < planes, 1.0, gate)

        def tile(at, size):
            got = mm(hot, gt[i, yy, :, pl.ds(at, size)], 1, 0) * gate
            got = got.astype(BF16)
            sx[i, yy * cap : (yy + 1) * cap, pl.ds(at, size)] = got[:cap]
            rows[i, yy * cap : (yy + 1) * cap, pl.ds(at, size)] = got[cap:]

        tiles(feat, 512, tile)
        x_copy(i, yy).start()

        @pl.when(i < planes)
        def _():
            mx_copy(i, yy).start()

    def stage_z(i):
        @pl.when(i == 0)
        def _():
            tok_in.wait()

        @pl.when(i == count - 1)
        def _():
            dmix_in.wait()

        @pl.when(ring_of(i) != 0)
        def _():
            z_copy(i, tok).wait_recv()

            @pl.when(i < planes)
            def _():
                mz_copy(i).wait_recv()

        y_copy(i).start()

        @pl.when(i < planes)
        def _():
            my_copy(i).start()

        @pl.when(i < planes - 1)
        def _():
            z_copy(i + planes, dmix).start()

    def stage_y(i):
        y_copy(i).wait()

        @pl.when(i < planes)
        def _():
            my_copy(i).wait()

        select(i, 1)

    def stage_in(i):
        for yy in range(2):
            x_copy(i, yy).wait()

        @pl.when(i < planes)
        def _():
            for yy in range(2):
                mx_copy(i, yy).wait()

            @pl.when(i == 0)
            def _():
                wu_in.wait()

            def tile(at, size):
                part[i % 2, :, pl.ds(at, size)] = mm(
                    rows[i], wu[:, pl.ds(at, size)], 1, 0
                ).astype(BF16)

            tiles(ff, 256, tile)

        @pl.when(i >= planes)
        def _():
            def tile(at, size):
                part[i % 2, :, pl.ds(at, size)] = mm(
                    rows[i], wd[pl.ds(at, size), :], 1, 1
                ).astype(BF16)

            tiles(ff, 256, tile)

        for o in range(1, nd):
            rs_copy(i, o).start()

    def stage_act(i):
        for o in range(1, nd):
            rs_copy(i, o).wait()
        r = ring_of(i)
        base = me * share

        def tile(at, size):
            here = pl.ds(pl.multiple_of(base + at, size), size)
            total = part[i % 2, here, :].astype(F32)
            for o in range(1, nd):
                total = total + rsbuf[i, o - 1, pl.ds(at, size), :].astype(F32)

            @pl.when(i < planes)
            def _():
                pre[r, pl.ds(at, size), :] = total
                hid[i, here, :] = (total / (1.0 + jnp.exp(-total))).astype(BF16)

            @pl.when(i >= planes)
            def _():
                value = pre[r, pl.ds(at, size), :]
                s = 1.0 / (1.0 + jnp.exp(-value))
                hid[i, here, :] = (total * s * (1.0 + value * (1.0 - s))).astype(BF16)

        tiles(share, 16, tile)
        for o in range(1, nd):
            ag_copy(i, o).start()

    def stage_out(i):
        for o in range(1, nd):
            ag_copy(i, o).wait()

        def store(at, size, got):
            got = got.astype(BF16)
            own[i % 2, :, pl.ds(at, size)] = got[:half]
            sx[i, :, pl.ds(at, size)] = got[half:]

        @pl.when(i < planes)
        def _():
            @pl.when(i == 0)
            def _():
                wd_in.wait()

            gate = jnp.concatenate(
                [pick(t.at[i, yy], e)[1] for t in (mt, mx) for yy in range(2)], 0
            )

            def tile(at, size):
                store(at, size, mm(hid[i], wd[:, pl.ds(at, size)], 1, 0) * gate)

            tiles(feat, 256, tile)

        @pl.when(i >= planes)
        def _():
            def tile(at, size):
                store(at, size, mm(hid[i], wu[pl.ds(at, size), :], 1, 1))

            tiles(feat, 256, tile)

        cx_copy(i).start()

    def stage_cx(i):
        cx_copy(i).wait()
        r = ring_of(i)
        for yy in (1, 0):
            hot = jnp.concatenate([pick(mt.at[r, yy], e)[0], pick(mt.at[r, yy], e_x)[0]], 0)

            def tile(at, size):
                there = slice(yy * cap, (yy + 1) * cap)
                data = jnp.concatenate(
                    [own[i % 2, there, pl.ds(at, size)], cx[i, there, pl.ds(at, size)]], 0
                )
                gt[i, yy, :, pl.ds(at, size)] = mm(hot, data, 0, 0).astype(BF16)

            tiles(feat, 512, tile)
            if yy == 1:
                cy_copy(i).start()

    def stage_cy(i):
        cy_copy(i).wait()

        def tile(at, size):
            here = pl.ds(at, size)
            total = gt[i, 0, here, :].astype(F32) + cy[i, here, :].astype(F32)
            gt[i, 0, here, :] = total.astype(BF16)

        tiles(t_rows, 16, tile)

        @pl.when(ring_of(i) != 0)
        def _():
            cz_copy(i).start()

    def finish(kind, out):
        far = range(1, planes) if kind == 0 else range(planes, count - 1)
        near = 0 if kind == 0 else count - 1
        for i in far:
            cz_copy(i).wait()

        def tile(at, size):
            here = pl.ds(at, size)
            total = gt[near, 0, here, :].astype(F32)
            for i in far:
                total = total + cz[i, here, :].astype(F32)
            out[here, :] = total.astype(BF16)

        tiles(t_rows, 16, tile)

    def live(i, body):
        @pl.when(jnp.logical_and(i >= 0, i < count))
        def _():
            body(i)

    def tick(i, carry):
        live(i, stage_z)
        live(i - 1, stage_y)
        live(i, lambda i: select(i, 0))
        live(i - 4, stage_out)
        live(i - 3, stage_act)
        live(i - 2, stage_in)
        live(i - 6, stage_cy)
        live(i - 5, stage_cx)
        return carry

    lax.fori_loop(0, count + 4, tick, 0)

    pairs = [((i + 1) % planes, i + planes) for i in range(planes)]

    def down_tile(at, size):
        total = None
        for a, b in pairs:
            term = mm(hid[a, :, pl.ds(at, size)], rows[b], 0, 0)
            total = term if total is None else total + term
        wd[pl.ds(at, size), :] = total.astype(BF16)

    tiles(ff, 128, down_tile)
    down_out = pltpu.make_async_copy(wd, grad_down.at[0], loc.at[3])
    down_out.start()

    stage_cy(count - 2)
    stage_cx(count - 1)

    def up_tile(at, size):
        total = None
        for a, b in pairs:
            term = mm(rows[a, :, pl.ds(at, size)], hid[b], 0, 0)
            total = term if total is None else total + term
        wu[pl.ds(at, size), :] = total.astype(BF16)

    tiles(feat, 256, up_tile)
    up_out = pltpu.make_async_copy(wu, grad_up.at[0], loc.at[2])
    up_out.start()

    stage_cy(count - 1)
    finish(0, mixed)
    finish(1, dtok)
    for i in range(1, planes):
        z_copy(i, tok).wait_send()
        mz_copy(i).wait_send()
    for i in range(planes, count - 1):
        z_copy(i, dmix).wait_send()
    down_out.wait()
    up_out.wait()


def per_device(tokens, gates, expert_ids, d_mixed, w_up, w_down):
    t_rows, feat = tokens.shape
    top = expert_ids.shape[1]
    ff = w_up.shape[2]
    groups = lax.axis_size("expert")
    nd = lax.axis_size("dp")
    hot_rows = t_rows // 2
    cold_rows = (t_rows * top - hot_rows + groups - 2) // (groups - 1)
    cap = max(hot_rows, cold_rows)
    planes = groups // 4
    count = 2 * planes
    half, chunk = 2 * cap, 4 * cap
    share = chunk // nd
    cfg = (groups, nd, t_rows, top, feat, ff, cap)
    dma = pltpu.SemaphoreType.DMA
    vm = pltpu.VMEM
    scratch = [
        vm((count, 2, t_rows, feat), BF16),
        vm((count, half, feat), BF16),
        vm((count, chunk, feat), BF16),
        vm((feat, ff), BF16),
        vm((ff, feat), BF16),
        vm((2, chunk, ff), BF16),
        vm((count, nd - 1, share, ff), BF16),
        vm((count, chunk, ff), BF16),
        vm((planes, share, ff), F32),
        vm((2, half, feat), BF16),
        vm((count, half, feat), BF16),
        vm((count, t_rows, feat), BF16),
        vm((count, t_rows, feat), BF16),
        vm((planes, 2, 2 * groups, t_rows), F32),
        vm((planes, 2, 2 * groups, t_rows), F32),
    ]
    for shape in (
        [(count,)] * 2 + [(planes,)] * 2 + [(count,)] * 2 + [(planes,)] * 2
        + [(count, 2)] * 2 + [(planes, 2)] * 2 + [(count, nd - 1)] * 4 + [(count,)] * 6 + [(4,)]
    ):
        scratch.append(dma(shape))
    pairs = groups * cap
    space = pl.BlockSpec(memory_space=pl.ANY)
    vmem = pl.BlockSpec(memory_space=pltpu.VMEM)
    return pl.pallas_call(
        functools.partial(kernel, cfg),
        out_shape=(
            jax.ShapeDtypeStruct((t_rows, feat), BF16),
            jax.ShapeDtypeStruct((t_rows, feat), BF16),
            jax.ShapeDtypeStruct(w_up.shape, BF16),
            jax.ShapeDtypeStruct(w_down.shape, BF16),
        ),
        in_specs=[space, vmem, vmem, space, space, space],
        out_specs=(vmem, vmem, space, space),
        scratch_shapes=scratch,
        compiler_params=pltpu.CompilerParams(
            collective_id=0, has_side_effects=True, vmem_limit_bytes=60 * 2**20
        ),
        cost_estimate=pl.CostEstimate(
            flops=12 * pairs * feat * ff, bytes_accessed=8 * feat * ff, transcendentals=pairs * ff
        ),
        name="moe_layer",
    )(tokens, gates, expert_ids, d_mixed, w_up, w_down)


def solution(mesh):
    in_specs = (
        P("expert", "dp"),
        P("expert", None),
        P("expert", None),
        P("expert", "dp"),
        P("expert", "dp", None),
        P("expert", None, "dp"),
    )
    out_specs = (
        P("expert", "dp"),
        P("expert", "dp"),
        P("expert", "dp", None),
        P("expert", None, "dp"),
    )
    return jax.shard_map(
        per_device, mesh=mesh, in_specs=in_specs, out_specs=out_specs, check_vma=False
    )
```

```python
import functools

import jax
import jax.numpy as jnp
from jax import lax
from jax.experimental import pallas as pl
from jax.experimental.pallas import tpu as pltpu
from jax.sharding import PartitionSpec as P

MESH = pl.DeviceIdType.MESH
F32 = jnp.float32
BF16 = jnp.bfloat16


def tiles(extent, size, body):
    size = min(size, extent)

    def step(j, carry):
        body(pl.multiple_of(j * size, size), size)
        return carry

    lax.fori_loop(0, extent // size, step, 0)


def flip(value, mask, limit):
    result = value
    bit = 1
    while bit < limit:
        on = (mask // bit) % 2
        result = result + bit * on * (1 - 2 * ((value // bit) % 2))
        bit *= 2
    return result


def differ(a, b, limit):
    result = 0
    bit = 1
    while bit < limit:
        result = result + bit * ((a // bit + b // bit) % 2)
        bit *= 2
    return result


def mm(a, b, da, db):
    return lax.dot_general(a, b, (((da,), (db,)), ((), ())), preferred_element_type=F32)


def kernel(
    cfg,
    tok, gates, ids, dmix, w_up, w_down,
    mixed, dtok, grad_up, grad_down,
    gt, sx, rows, wu, wd, part, rsbuf, hid, pre, own, cx, cy, cz, mt, mx,
    zs, zr, mzs, mzr, ys, yr, mys, myr, xs, xr, mxs, mxr,
    rss, rsr, ags, agr, cxs, cxr, cys, cyr, czs, czr, loc,
):
    groups, nd, t_rows, top, feat, ff, cap = cfg
    planes = groups // 4
    count = 2 * planes
    half = 2 * cap
    chunk = 4 * cap
    share = chunk // nd
    e = lax.axis_index("expert")
    me = lax.axis_index("dp")
    z, y, x = e // 4, (e // 2) % 2, e % 2
    e_x = e + 1 - 2 * x
    e_y = e + 2 - 4 * y

    def ring_of(i):
        r = (i + i // planes) % planes
        if planes == 4:
            inner = (z % 3 + 2) // 3
            r = r + inner * (r // 2) * (5 - 2 * r)
        return r

    def slot_of(i):
        return (i // planes) * planes + ring_of(i)

    def z_peer(r):
        return flip(z, r, planes) * 4 + y * 2 + x

    def send(src, dst, ssem, rsem, expert=None, dp=None):
        where = {"expert": expert} if dp is None else {"dp": dp}
        return pltpu.make_async_remote_copy(
            src_ref=src, dst_ref=dst, send_sem=ssem, recv_sem=rsem,
            device_id=where, device_id_type=MESH,
        )

    def z_next(s, origin, way):
        there = z + 1 - 2 * way
        return there * 4 + y * 2 + x, (s // planes) * planes + differ(origin, there, planes)

    def z_copy(s, origin, way, src=None):
        peer, slot = z_next(s, origin, way)
        src = gt.at[s, 0] if src is None else src
        return send(src, gt.at[slot, 0], zs.at[s, way], zr.at[slot], peer)

    def mz_copy(s, origin, way):
        peer, slot = z_next(s, origin, way)
        return send(mt.at[s, 0], mt.at[slot, 0], mzs.at[s, way], mzr.at[slot], peer)

    def onward(s, act):
        origin = flip(z, s % planes, planes)

        @pl.when(jnp.logical_and(origin < z, z < planes - 1))
        def _():
            act(origin, 0)

        @pl.when(jnp.logical_and(origin > z, z > 0))
        def _():
            act(origin, 1)

    def outward(act):
        @pl.when(z < planes - 1)
        def _():
            act(z, 0)

        @pl.when(z > 0)
        def _():
            act(z, 1)

    def y_copy(i):
        return send(gt.at[i, 0], gt.at[i, 1], ys.at[i], yr.at[i], e_y)

    def my_copy(i):
        return send(mt.at[i, 0], mt.at[i, 1], mys.at[i], myr.at[i], e_y)

    def x_copy(i, yy):
        return send(
            sx.at[i, pl.ds(yy * cap, cap)], rows.at[i, pl.ds(half + yy * cap, cap)],
            xs.at[i, yy], xr.at[i, yy], e_x,
        )

    def mx_copy(i, yy):
        return send(mt.at[i, yy], mx.at[i, yy], mxs.at[i, yy], mxr.at[i, yy], e_x)

    def rs_copy(i, h, o):
        peer = (me + o) % nd
        return send(
            part.at[h, pl.ds(pl.multiple_of(peer * share, share), share)],
            rsbuf.at[i, o - 1], rss.at[i, o - 1], rsr.at[i, o - 1], dp=peer,
        )

    def ag_copy(i, o):
        mine = hid.at[i, pl.ds(pl.multiple_of(me * share, share), share)]
        return send(mine, mine, ags.at[i, o - 1], agr.at[i, o - 1], dp=(me + o) % nd)

    def cx_copy(i, yy):
        here = pl.ds(yy * cap, cap)
        return send(sx.at[i, here], cx.at[i, here], cxs.at[i, yy], cxr.at[i, yy], e_x)

    def cy_copy(i):
        return send(gt.at[i, 1], cy.at[i], cys.at[i], cyr.at[i], e_y)

    def cz_copy(i):
        return send(gt.at[i, 0], cz.at[i], czs.at[i], czr.at[i], z_peer(i % planes))

    tok_in = pltpu.make_async_copy(tok, gt.at[0, 0], loc.at[0])
    dmix_in = pltpu.make_async_copy(dmix, gt.at[planes, 0], loc.at[1])
    wu_in = pltpu.make_async_copy(w_up.at[0], wu, loc.at[2])
    wd_in = pltpu.make_async_copy(w_down.at[0], wd, loc.at[3])
    tok_in.start()
    dmix_in.start()
    wu_in.start()
    wd_in.start()

    barrier = pltpu.get_barrier_semaphore()
    peers = [{"expert": z_peer(r)} for r in range(1, planes)]
    peers += [{"expert": e_x}, {"expert": e_y}]
    peers += [{"dp": (me + o) % nd} for o in range(1, nd)]
    for peer in peers:
        pl.semaphore_signal(barrier, inc=1, device_id=peer, device_id_type=MESH)
    pl.semaphore_wait(barrier, len(peers))

    outward(lambda origin, way: z_copy(0, origin, way, tok).start())

    expert_row = lax.broadcasted_iota(jnp.int32, (groups, t_rows), 0)
    chosen = jnp.zeros((groups, t_rows), F32)
    weight = jnp.zeros((groups, t_rows), F32)
    for k in range(top):
        hit = ids[k : k + 1, :] == expert_row
        chosen = chosen + jnp.where(hit, 1.0, 0.0)
        weight = weight + jnp.where(hit, gates[k : k + 1, :], 0.0)
    lane = lax.broadcasted_iota(jnp.int32, (t_rows, t_rows), 1)
    row = lax.broadcasted_iota(jnp.int32, (t_rows, t_rows), 0)
    before = jnp.where(row < lane, 1.0, 0.0).astype(BF16)
    place = mm(chosen.astype(BF16), before, 1, 0)
    mt[0, 0, :groups, :] = jnp.where(chosen > 0.0, place, -1.0)
    mt[0, 0, groups:, :] = weight
    outward(lambda origin, way: mz_copy(0, origin, way).start())

    slot = lax.broadcasted_iota(jnp.int32, (cap, t_rows), 0).astype(F32)

    def pick(table, expert):
        hot = slot == table[pl.ds(expert, 1), :]
        gate = jnp.sum(jnp.where(hot, table[pl.ds(groups + expert, 1), :], 0.0), 1, keepdims=True)
        return jnp.where(hot, 1.0, 0.0).astype(BF16), gate

    def select(i, yy):
        r = i % planes
        hot_n, gate_n = pick(mt.at[r, yy], e_x)
        hot_o, gate_o = pick(mt.at[r, yy], e)
        hot = jnp.concatenate([hot_n, hot_o], 0)
        gate = jnp.concatenate([gate_n, gate_o], 0)
        gate = jnp.where(i < planes, 1.0, gate)

        def tile(at, size):
            got = mm(hot, gt[i, yy, :, pl.ds(at, size)], 1, 0) * gate
            got = got.astype(BF16)
            sx[i, yy * cap : (yy + 1) * cap, pl.ds(at, size)] = got[:cap]
            rows[i, yy * cap : (yy + 1) * cap, pl.ds(at, size)] = got[cap:]

        tiles(feat, 512, tile)
        x_copy(i, yy).start()

        @pl.when(i < planes)
        def _():
            mx_copy(i, yy).start()

    def stage_z(i):
        @pl.when(i == 0)
        def _():
            tok_in.wait()

        @pl.when(i == planes)
        def _():
            dmix_in.wait()

        @pl.when(i % planes != 0)
        def _():
            send(gt.at[i, 0], gt.at[i, 0], zs.at[i, 0], zr.at[i], e_x).wait_recv()
            onward(i, lambda origin, way: z_copy(i, origin, way).start())

            @pl.when(i < planes)
            def _():
                send(mt.at[i, 0], mt.at[i, 0], mzs.at[i, 0], mzr.at[i], e_x).wait_recv()
                onward(i, lambda origin, way: mz_copy(i, origin, way).start())

        y_copy(i).start()

        @pl.when(i < planes)
        def _():
            my_copy(i).start()

        @pl.when(i == 1)
        def _():
            outward(lambda origin, way: z_copy(planes, origin, way, dmix).start())

    def stage_y(i):
        y_copy(i).wait()

        @pl.when(i < planes)
        def _():
            my_copy(i).wait()

        select(i, 1)

    def stage_in(i, h):
        for yy in range(2):
            x_copy(i, yy).wait()

        @pl.when(i < planes)
        def _():
            for yy in range(2):
                mx_copy(i, yy).wait()

            @pl.when(i == 0)
            def _():
                wu_in.wait()

            def tile(at, size):
                part[h, :, pl.ds(at, size)] = mm(
                    rows[i], wu[:, pl.ds(at, size)], 1, 0
                ).astype(BF16)

            tiles(ff, 256, tile)

        @pl.when(i >= planes)
        def _():
            def tile(at, size):
                part[h, :, pl.ds(at, size)] = mm(
                    rows[i], wd[pl.ds(at, size), :], 1, 1
                ).astype(BF16)

            tiles(ff, 256, tile)

        for o in range(1, nd):
            rs_copy(i, h, o).start()

    def stage_act(i, h):
        for o in range(1, nd):
            rs_copy(i, h, o).wait()
        r = i % planes
        base = me * share

        def tile(at, size):
            here = pl.ds(pl.multiple_of(base + at, size), size)
            total = part[h, here, :].astype(F32)
            for o in range(1, nd):
                total = total + rsbuf[i, o - 1, pl.ds(at, size), :].astype(F32)

            @pl.when(i < planes)
            def _():
                pre[r, pl.ds(at, size), :] = total
                hid[i, here, :] = (total / (1.0 + jnp.exp(-total))).astype(BF16)

            @pl.when(i >= planes)
            def _():
                value = pre[r, pl.ds(at, size), :]
                s = 1.0 / (1.0 + jnp.exp(-value))
                hid[i, here, :] = (total * s * (1.0 + value * (1.0 - s))).astype(BF16)

        tiles(share, 16, tile)
        for o in range(1, nd):
            ag_copy(i, o).start()

    def stage_out(i, h):
        for o in range(1, nd):
            ag_copy(i, o).wait()

        def store(at, size, got):
            got = got.astype(BF16)
            own[h, :, pl.ds(at, size)] = got[:half]
            sx[i, :, pl.ds(at, size)] = got[half:]

        @pl.when(i < planes)
        def _():
            @pl.when(i == 0)
            def _():
                wd_in.wait()

            gate = jnp.concatenate(
                [pick(t.at[i, yy], e)[1] for t in (mt, mx) for yy in range(2)], 0
            )

            def tile(at, size):
                store(at, size, mm(hid[i], wd[:, pl.ds(at, size)], 1, 0) * gate)

            tiles(feat, 256, tile)

        @pl.when(i >= planes)
        def _():
            def tile(at, size):
                store(at, size, mm(hid[i], wu[pl.ds(at, size), :], 1, 1))

            tiles(feat, 256, tile)

        cx_copy(i, 1).start()
        cx_copy(i, 0).start()

    def placed(i, h, yy):
        r = i % planes
        hot = jnp.concatenate([pick(mt.at[r, yy], e)[0], pick(mt.at[r, yy], e_x)[0]], 0)
        there = slice(yy * cap, (yy + 1) * cap)

        def tile(at, size):
            data = jnp.concatenate(
                [own[h, there, pl.ds(at, size)], cx[i, there, pl.ds(at, size)]], 0
            )
            return mm(hot, data, 0, 0)

        return tile

    def stage_cx(i, h):
        cx_copy(i, 1).wait()
        sums = placed(i, h, 1)

        def tile(at, size):
            gt[i, 1, :, pl.ds(at, size)] = sums(at, size).astype(BF16)

        tiles(feat, 512, tile)
        cy_copy(i).start()

    def stage_cy(i, h):
        cx_copy(i, 0).wait()
        cy_copy(i).wait()

        @pl.when(i % planes != 0)
        def _():
            onward(i, lambda origin, way: z_copy(i, origin, way).wait_send())

        sums = placed(i, h, 0)

        def tile(at, size):
            here = pl.ds(at, size)
            gt[i, 0, :, here] = (sums(at, size) + cy[i, :, here].astype(F32)).astype(BF16)

        tiles(feat, 512, tile)

        @pl.when(i % planes != 0)
        def _():
            cz_copy(i).start()

    def finish(kind, out):
        near = kind * planes
        far = range(near + 1, near + planes)
        for i in far:
            cz_copy(i).wait()

        def tile(at, size):
            here = pl.ds(at, size)
            total = gt[near, 0, here, :].astype(F32)
            for i in far:
                total = total + cz[i, here, :].astype(F32)
            out[here, :] = total.astype(BF16)

        tiles(t_rows, 16, tile)

    def live(i, body):
        @pl.when(jnp.logical_and(i >= 0, i < count))
        def _():
            body(slot_of(i), i % 2)

    def tick(i, carry):
        live(i - 6, stage_cy)
        live(i - 5, stage_cx)
        live(i - 4, stage_act)
        live(i - 4, stage_out)
        live(i - 2, lambda s, h: stage_y(s))
        live(i - 3, stage_in)
        live(i, lambda s, h: stage_z(s))
        live(i, lambda s, h: select(s, 0))
        return carry

    lax.fori_loop(0, count + 4, tick, 0)

    pairs = [(i, i + planes) for i in range(planes)]

    def down_tile(at, size):
        total = None
        for a, b in pairs:
            term = mm(hid[a, :, pl.ds(at, size)], rows[b], 0, 0)
            total = term if total is None else total + term
        wd[pl.ds(at, size), :] = total.astype(BF16)

    tiles(ff, 128, down_tile)
    down_out = pltpu.make_async_copy(wd, grad_down.at[0], loc.at[3])
    down_out.start()

    stage_cy(slot_of(count - 2), count % 2)
    stage_cx(slot_of(count - 1), (count - 1) % 2)

    def up_tile(at, size):
        total = None
        for a, b in pairs:
            term = mm(rows[a, :, pl.ds(at, size)], hid[b], 0, 0)
            total = term if total is None else total + term
        wu[pl.ds(at, size), :] = total.astype(BF16)

    tiles(feat, 256, up_tile)
    up_out = pltpu.make_async_copy(wu, grad_up.at[0], loc.at[2])
    up_out.start()

    stage_cy(slot_of(count - 1), (count - 1) % 2)
    finish(0, mixed)
    finish(1, dtok)
    outward(lambda origin, way: z_copy(0, origin, way, tok).wait_send())
    outward(lambda origin, way: z_copy(planes, origin, way, dmix).wait_send())
    outward(lambda origin, way: mz_copy(0, origin, way).wait_send())
    for i in range(1, planes):
        onward(i, lambda origin, way, i=i: mz_copy(i, origin, way).wait_send())
    down_out.wait()
    up_out.wait()


def per_device(tokens, gates, expert_ids, d_mixed, w_up, w_down):
    t_rows, feat = tokens.shape
    top = expert_ids.shape[1]
    ff = w_up.shape[2]
    groups = lax.axis_size("expert")
    nd = lax.axis_size("dp")
    hot_rows = t_rows // 2
    cold_rows = (t_rows * top - hot_rows + groups - 2) // (groups - 1)
    cap = max(hot_rows, cold_rows)
    planes = groups // 4
    count = 2 * planes
    half, chunk = 2 * cap, 4 * cap
    share = chunk // nd
    cfg = (groups, nd, t_rows, top, feat, ff, cap)
    dma = pltpu.SemaphoreType.DMA
    vm = pltpu.VMEM
    scratch = [
        vm((count, 2, t_rows, feat), BF16),
        vm((count, half, feat), BF16),
        vm((count, chunk, feat), BF16),
        vm((feat, ff), BF16),
        vm((ff, feat), BF16),
        vm((2, chunk, ff), BF16),
        vm((count, nd - 1, share, ff), BF16),
        vm((count, chunk, ff), BF16),
        vm((planes, share, ff), F32),
        vm((2, half, feat), BF16),
        vm((count, half, feat), BF16),
        vm((count, t_rows, feat), BF16),
        vm((count, t_rows, feat), BF16),
        vm((planes, 2, 2 * groups, t_rows), F32),
        vm((planes, 2, 2 * groups, t_rows), F32),
    ]
    for shape in (
        [(count, 2), (count,), (planes, 2), (planes,)] + [(count,)] * 2 + [(planes,)] * 2
        + [(count, 2)] * 2 + [(planes, 2)] * 2 + [(count, nd - 1)] * 4 + [(count, 2)] * 2 + [(count,)] * 4 + [(4,)]
    ):
        scratch.append(dma(shape))
    pairs = groups * cap
    space = pl.BlockSpec(memory_space=pl.ANY)
    vmem = pl.BlockSpec(memory_space=pltpu.VMEM)
    return pl.pallas_call(
        functools.partial(kernel, cfg),
        out_shape=(
            jax.ShapeDtypeStruct((t_rows, feat), BF16),
            jax.ShapeDtypeStruct((t_rows, feat), BF16),
            jax.ShapeDtypeStruct(w_up.shape, BF16),
            jax.ShapeDtypeStruct(w_down.shape, BF16),
        ),
        in_specs=[space, vmem, vmem, space, space, space],
        out_specs=(vmem, vmem, space, space),
        scratch_shapes=scratch,
        compiler_params=pltpu.CompilerParams(
            collective_id=0, has_side_effects=True, vmem_limit_bytes=60 * 2**20
        ),
        cost_estimate=pl.CostEstimate(
            flops=12 * pairs * feat * ff, bytes_accessed=8 * feat * ff, transcendentals=pairs * ff
        ),
        name="moe_layer",
    )(tokens, gates.T, expert_ids.T, d_mixed, w_up, w_down)


def solution(mesh):
    in_specs = (
        P("expert", "dp"),
        P("expert", None),
        P("expert", None),
        P("expert", "dp"),
        P("expert", "dp", None),
        P("expert", None, "dp"),
    )
    out_specs = (
        P("expert", "dp"),
        P("expert", "dp"),
        P("expert", "dp", None),
        P("expert", None, "dp"),
    )
    return jax.shard_map(
        per_device, mesh=mesh, in_specs=in_specs, out_specs=out_specs, check_vma=False
    )
```

```python
import functools

import jax
import jax.numpy as jnp
from jax import lax
from jax.experimental import pallas as pl
from jax.experimental.pallas import tpu as pltpu
from jax.sharding import PartitionSpec as P

MESH = pl.DeviceIdType.MESH
F32 = jnp.float32
BF16 = jnp.bfloat16


def tiles(extent, size, body):
    size = min(size, extent)

    def step(j, carry):
        body(pl.multiple_of(j * size, size), size)
        return carry

    lax.fori_loop(0, extent // size, step, 0)


def flip(value, mask, limit):
    result = value
    bit = 1
    while bit < limit:
        on = (mask // bit) % 2
        result = result + bit * on * (1 - 2 * ((value // bit) % 2))
        bit *= 2
    return result


def differ(a, b, limit):
    result = 0
    bit = 1
    while bit < limit:
        result = result + bit * ((a // bit + b // bit) % 2)
        bit *= 2
    return result


def mm(a, b, da, db):
    return lax.dot_general(a, b, (((da,), (db,)), ((), ())), preferred_element_type=F32)


def kernel(
    cfg,
    tok, gates, ids, dmix, w_up, w_down,
    mixed, dtok, grad_up, grad_down,
    gt, sx, rows, wu, wd, part, rsbuf, hid, pre, own, cx, cy, cz, mt, mx,
    zs, zr, mzs, mzr, ys, yr, mys, myr, xs, xr, mxs, mxr,
    rss, rsr, ags, agr, cxs, cxr, cys, cyr, czs, czr, loc,
):
    groups, nd, t_rows, top, feat, ff, cap = cfg
    planes = groups // 4
    count = 2 * planes
    half = 2 * cap
    chunk = 4 * cap
    share = chunk // nd
    e = lax.axis_index("expert")
    me = lax.axis_index("dp")
    z, y, x = e // 4, (e // 2) % 2, e % 2
    e_x = e + 1 - 2 * x
    e_y = e + 2 - 4 * y

    def ring_of(i):
        kind, m = i // planes, i % planes
        r = (m + kind) % planes
        if planes == 4:
            r = m + kind * (2 - 2 * m + (m // 2) * (3 - 2 * (m % 2)))
            inner = (z % 3 + 2) // 3
            r = r + inner * (r // 2) * (5 - 2 * r)
        return r

    def slot_of(i):
        return (i // planes) * planes + ring_of(i)

    def z_peer(r):
        return flip(z, r, planes) * 4 + y * 2 + x

    def send(src, dst, ssem, rsem, expert=None, dp=None):
        where = {"expert": expert} if dp is None else {"dp": dp}
        return pltpu.make_async_remote_copy(
            src_ref=src, dst_ref=dst, send_sem=ssem, recv_sem=rsem,
            device_id=where, device_id_type=MESH,
        )

    def z_next(s, origin, way):
        there = z + 1 - 2 * way
        return there * 4 + y * 2 + x, (s // planes) * planes + differ(origin, there, planes)

    def z_copy(s, origin, way, src=None):
        peer, slot = z_next(s, origin, way)
        src = gt.at[s, 0] if src is None else src
        return send(src, gt.at[slot, 0], zs.at[s, way], zr.at[slot], peer)

    def mz_copy(s, origin, way):
        peer, slot = z_next(s, origin, way)
        return send(mt.at[s, 0], mt.at[slot, 0], mzs.at[s, way], mzr.at[slot], peer)

    def onward(s, act):
        origin = flip(z, s % planes, planes)

        @pl.when(jnp.logical_and(origin < z, z < planes - 1))
        def _():
            act(origin, 0)

        @pl.when(jnp.logical_and(origin > z, z > 0))
        def _():
            act(origin, 1)

    def outward(act):
        @pl.when(z < planes - 1)
        def _():
            act(z, 0)

        @pl.when(z > 0)
        def _():
            act(z, 1)

    def y_copy(i):
        return send(gt.at[i, 0], gt.at[i, 1], ys.at[i], yr.at[i], e_y)

    def my_copy(i):
        return send(mt.at[i, 0], mt.at[i, 1], mys.at[i], myr.at[i], e_y)

    def x_copy(i, yy):
        return send(
            sx.at[i, pl.ds(yy * cap, cap)], rows.at[i, pl.ds(half + yy * cap, cap)],
            xs.at[i, yy], xr.at[i, yy], e_x,
        )

    def mx_copy(i, yy):
        return send(mt.at[i, yy], mx.at[i, yy], mxs.at[i, yy], mxr.at[i, yy], e_x)

    def rs_copy(i, h, o):
        peer = (me + o) % nd
        return send(
            part.at[h, pl.ds(pl.multiple_of(peer * share, share), share)],
            rsbuf.at[i, o - 1], rss.at[i, o - 1], rsr.at[i, o - 1], dp=peer,
        )

    def ag_copy(i, o):
        mine = hid.at[i, pl.ds(pl.multiple_of(me * share, share), share)]
        return send(mine, mine, ags.at[i, o - 1], agr.at[i, o - 1], dp=(me + o) % nd)

    def cx_copy(i, yy):
        here = pl.ds(yy * cap, cap)
        return send(sx.at[i, here], cx.at[i, here], cxs.at[i, yy], cxr.at[i, yy], e_x)

    def cy_copy(i):
        return send(gt.at[i, 1], cy.at[i], cys.at[i], cyr.at[i], e_y)

    def cz_copy(i):
        return send(gt.at[i, 0], cz.at[i], czs.at[i], czr.at[i], z_peer(i % planes))

    tok_in = pltpu.make_async_copy(tok, gt.at[0, 0], loc.at[0])
    dmix_in = pltpu.make_async_copy(dmix, gt.at[planes, 0], loc.at[1])
    wu_in = pltpu.make_async_copy(w_up.at[0], wu, loc.at[2])
    wd_in = pltpu.make_async_copy(w_down.at[0], wd, loc.at[3])
    tok_in.start()
    dmix_in.start()
    wu_in.start()
    wd_in.start()

    barrier = pltpu.get_barrier_semaphore()
    peers = [{"expert": z_peer(r)} for r in range(1, planes)]
    peers += [{"expert": e_x}, {"expert": e_y}]
    peers += [{"dp": (me + o) % nd} for o in range(1, nd)]
    for peer in peers:
        pl.semaphore_signal(barrier, inc=1, device_id=peer, device_id_type=MESH)
    pl.semaphore_wait(barrier, len(peers))

    outward(lambda origin, way: z_copy(0, origin, way, tok).start())

    expert_row = lax.broadcasted_iota(jnp.int32, (groups, t_rows), 0)
    chosen = jnp.zeros((groups, t_rows), F32)
    weight = jnp.zeros((groups, t_rows), F32)
    for k in range(top):
        hit = ids[k : k + 1, :] == expert_row
        chosen = chosen + jnp.where(hit, 1.0, 0.0)
        weight = weight + jnp.where(hit, gates[k : k + 1, :], 0.0)
    lane = lax.broadcasted_iota(jnp.int32, (t_rows, t_rows), 1)
    row = lax.broadcasted_iota(jnp.int32, (t_rows, t_rows), 0)
    before = jnp.where(row < lane, 1.0, 0.0).astype(BF16)
    place = mm(chosen.astype(BF16), before, 1, 0)
    mt[0, 0, :groups, :] = jnp.where(chosen > 0.0, place, -1.0)
    mt[0, 0, groups:, :] = weight
    outward(lambda origin, way: mz_copy(0, origin, way).start())

    slot = lax.broadcasted_iota(jnp.int32, (cap, t_rows), 0).astype(F32)

    def pick(table, expert):
        hot = slot == table[pl.ds(expert, 1), :]
        gate = jnp.sum(jnp.where(hot, table[pl.ds(groups + expert, 1), :], 0.0), 1, keepdims=True)
        return jnp.where(hot, 1.0, 0.0).astype(BF16), gate

    def select(i, yy):
        r = i % planes
        hot_n, gate_n = pick(mt.at[r, yy], e_x)
        hot_o, gate_o = pick(mt.at[r, yy], e)
        hot = jnp.concatenate([hot_n, hot_o], 0)
        gate = jnp.concatenate([gate_n, gate_o], 0)
        gate = jnp.where(i < planes, 1.0, gate)

        def tile(at, size):
            got = mm(hot, gt[i, yy, :, pl.ds(at, size)], 1, 0) * gate
            got = got.astype(BF16)
            sx[i, yy * cap : (yy + 1) * cap, pl.ds(at, size)] = got[:cap]
            rows[i, yy * cap : (yy + 1) * cap, pl.ds(at, size)] = got[cap:]

        tiles(feat, 512, tile)
        x_copy(i, yy).start()

        @pl.when(i < planes)
        def _():
            mx_copy(i, yy).start()

    def stage_z(i, order):
        @pl.when(i == 0)
        def _():
            tok_in.wait()

        @pl.when(i == planes)
        def _():
            dmix_in.wait()

        @pl.when(i % planes != 0)
        def _():
            send(gt.at[i, 0], gt.at[i, 0], zs.at[i, 0], zr.at[i], e_x).wait_recv()
            onward(i, lambda origin, way: z_copy(i, origin, way).start())

            @pl.when(i < planes)
            def _():
                send(mt.at[i, 0], mt.at[i, 0], mzs.at[i, 0], mzr.at[i], e_x).wait_recv()
                onward(i, lambda origin, way: mz_copy(i, origin, way).start())

        y_copy(i).start()

        @pl.when(i < planes)
        def _():
            my_copy(i).start()

        @pl.when(order == planes - 1)
        def _():
            outward(lambda origin, way: z_copy(planes, origin, way, dmix).start())

    def stage_y(i):
        y_copy(i).wait()

        @pl.when(i < planes)
        def _():
            my_copy(i).wait()

        select(i, 1)

    def stage_in(i, h):
        for yy in range(2):
            x_copy(i, yy).wait()

        @pl.when(i < planes)
        def _():
            for yy in range(2):
                mx_copy(i, yy).wait()

            @pl.when(i == 0)
            def _():
                wu_in.wait()

            def tile(at, size):
                part[h, :, pl.ds(at, size)] = mm(
                    rows[i], wu[:, pl.ds(at, size)], 1, 0
                ).astype(BF16)

            tiles(ff, 256, tile)

        @pl.when(i >= planes)
        def _():
            def tile(at, size):
                part[h, :, pl.ds(at, size)] = mm(
                    rows[i], wd[pl.ds(at, size), :], 1, 1
                ).astype(BF16)

            tiles(ff, 256, tile)

        for o in range(1, nd):
            rs_copy(i, h, o).start()

    def stage_act(i, h):
        for o in range(1, nd):
            rs_copy(i, h, o).wait()
        r = i % planes
        base = me * share

        def tile(at, size):
            here = pl.ds(pl.multiple_of(base + at, size), size)
            total = part[h, here, :].astype(F32)
            for o in range(1, nd):
                total = total + rsbuf[i, o - 1, pl.ds(at, size), :].astype(F32)

            @pl.when(i < planes)
            def _():
                pre[r, pl.ds(at, size), :] = total
                hid[i, here, :] = (total / (1.0 + jnp.exp(-total))).astype(BF16)

            @pl.when(i >= planes)
            def _():
                value = pre[r, pl.ds(at, size), :]
                s = 1.0 / (1.0 + jnp.exp(-value))
                hid[i, here, :] = (total * s * (1.0 + value * (1.0 - s))).astype(BF16)

        tiles(share, 16, tile)
        for o in range(1, nd):
            ag_copy(i, o).start()

    def stage_out(i, h):
        for o in range(1, nd):
            ag_copy(i, o).wait()

        def store(at, size, got):
            got = got.astype(BF16)
            own[h, :, pl.ds(at, size)] = got[:half]
            sx[i, :, pl.ds(at, size)] = got[half:]

        @pl.when(i < planes)
        def _():
            @pl.when(i == 0)
            def _():
                wd_in.wait()

            gate = jnp.concatenate(
                [pick(t.at[i, yy], e)[1] for t in (mt, mx) for yy in range(2)], 0
            )

            def tile(at, size):
                store(at, size, mm(hid[i], wd[:, pl.ds(at, size)], 1, 0) * gate)

            tiles(feat, 256, tile)

        @pl.when(i >= planes)
        def _():
            def tile(at, size):
                store(at, size, mm(hid[i], wu[pl.ds(at, size), :], 1, 1))

            tiles(feat, 256, tile)

        cx_copy(i, 1).start()
        cx_copy(i, 0).start()

    def placed(i, h, yy):
        r = i % planes
        hot = jnp.concatenate([pick(mt.at[r, yy], e)[0], pick(mt.at[r, yy], e_x)[0]], 0)
        there = slice(yy * cap, (yy + 1) * cap)

        def tile(at, size):
            data = jnp.concatenate(
                [own[h, there, pl.ds(at, size)], cx[i, there, pl.ds(at, size)]], 0
            )
            return mm(hot, data, 0, 0)

        return tile

    def stage_cx(i, h):
        cx_copy(i, 1).wait()
        sums = placed(i, h, 1)

        def tile(at, size):
            gt[i, 1, :, pl.ds(at, size)] = sums(at, size).astype(BF16)

        tiles(feat, 512, tile)
        cy_copy(i).start()

    def stage_cy(i, h):
        cx_copy(i, 0).wait()
        cy_copy(i).wait()

        @pl.when(i % planes != 0)
        def _():
            onward(i, lambda origin, way: z_copy(i, origin, way).wait_send())

        sums = placed(i, h, 0)

        def tile(at, size):
            here = pl.ds(at, size)
            gt[i, 0, :, here] = (sums(at, size) + cy[i, :, here].astype(F32)).astype(BF16)

        tiles(feat, 512, tile)

        @pl.when(i % planes != 0)
        def _():
            cz_copy(i).start()

    def finish(kind, out):
        near = kind * planes
        far = range(near + 1, near + planes)
        for i in far:
            cz_copy(i).wait()

        def tile(at, size):
            here = pl.ds(at, size)
            total = gt[near, 0, here, :].astype(F32)
            for i in far:
                total = total + cz[i, here, :].astype(F32)
            out[here, :] = total.astype(BF16)

        tiles(t_rows, 16, tile)

    def live(i, body):
        @pl.when(jnp.logical_and(i >= 0, i < count))
        def _():
            body(slot_of(i), i % 2)

    def tick(i, carry):
        live(i - 4, stage_act)
        live(i - 6, stage_cy)
        live(i - 5, stage_cx)
        live(i - 4, stage_out)
        live(i, lambda s, h: stage_z(s, i))
        live(i, lambda s, h: select(s, 0))
        live(i - 2, lambda s, h: stage_y(s))
        live(i - 3, stage_in)
        return carry

    lax.fori_loop(0, count + 4, tick, 0)

    pairs = [(i, i + planes) for i in range(planes)]

    def down_tile(at, size):
        total = None
        for a, b in pairs:
            term = mm(hid[a, :, pl.ds(at, size)], rows[b], 0, 0)
            total = term if total is None else total + term
        wd[pl.ds(at, size), :] = total.astype(BF16)

    tiles(ff, 256, down_tile)
    down_out = pltpu.make_async_copy(wd, grad_down.at[0], loc.at[3])
    down_out.start()

    stage_cy(slot_of(count - 2), count % 2)
    stage_cx(slot_of(count - 1), (count - 1) % 2)

    def up_tile(at, size):
        total = None
        for a, b in pairs:
            term = mm(rows[a, :, pl.ds(at, size)], hid[b], 0, 0)
            total = term if total is None else total + term
        wu[pl.ds(at, size), :] = total.astype(BF16)

    tiles(feat, 512, up_tile)
    up_out = pltpu.make_async_copy(wu, grad_up.at[0], loc.at[2])
    up_out.start()

    finish(0, mixed)
    stage_cy(slot_of(count - 1), (count - 1) % 2)
    finish(1, dtok)
    outward(lambda origin, way: z_copy(0, origin, way, tok).wait_send())
    outward(lambda origin, way: z_copy(planes, origin, way, dmix).wait_send())
    outward(lambda origin, way: mz_copy(0, origin, way).wait_send())
    for i in range(1, planes):
        onward(i, lambda origin, way, i=i: mz_copy(i, origin, way).wait_send())
    down_out.wait()
    up_out.wait()


def per_device(tokens, gates, expert_ids, d_mixed, w_up, w_down):
    t_rows, feat = tokens.shape
    top = expert_ids.shape[1]
    ff = w_up.shape[2]
    groups = lax.axis_size("expert")
    nd = lax.axis_size("dp")
    hot_rows = t_rows // 2
    cold_rows = (t_rows * top - hot_rows + groups - 2) // (groups - 1)
    cap = max(hot_rows, cold_rows)
    planes = groups // 4
    count = 2 * planes
    half, chunk = 2 * cap, 4 * cap
    share = chunk // nd
    cfg = (groups, nd, t_rows, top, feat, ff, cap)
    dma = pltpu.SemaphoreType.DMA
    vm = pltpu.VMEM
    scratch = [
        vm((count, 2, t_rows, feat), BF16),
        vm((count, half, feat), BF16),
        vm((count, chunk, feat), BF16),
        vm((feat, ff), BF16),
        vm((ff, feat), BF16),
        vm((2, chunk, ff), BF16),
        vm((count, nd - 1, share, ff), BF16),
        vm((count, chunk, ff), BF16),
        vm((planes, share, ff), F32),
        vm((2, half, feat), BF16),
        vm((count, half, feat), BF16),
        vm((count, t_rows, feat), BF16),
        vm((count, t_rows, feat), BF16),
        vm((planes, 2, 2 * groups, t_rows), F32),
        vm((planes, 2, 2 * groups, t_rows), F32),
    ]
    for shape in (
        [(count, 2), (count,), (planes, 2), (planes,)] + [(count,)] * 2 + [(planes,)] * 2
        + [(count, 2)] * 2 + [(planes, 2)] * 2 + [(count, nd - 1)] * 4 + [(count, 2)] * 2 + [(count,)] * 4 + [(4,)]
    ):
        scratch.append(dma(shape))
    pairs = groups * cap
    space = pl.BlockSpec(memory_space=pl.ANY)
    vmem = pl.BlockSpec(memory_space=pltpu.VMEM)
    return pl.pallas_call(
        functools.partial(kernel, cfg),
        out_shape=(
            jax.ShapeDtypeStruct((t_rows, feat), BF16),
            jax.ShapeDtypeStruct((t_rows, feat), BF16),
            jax.ShapeDtypeStruct(w_up.shape, BF16),
            jax.ShapeDtypeStruct(w_down.shape, BF16),
        ),
        in_specs=[space, vmem, vmem, space, space, space],
        out_specs=(vmem, vmem, space, space),
        scratch_shapes=scratch,
        compiler_params=pltpu.CompilerParams(
            collective_id=0, has_side_effects=True, vmem_limit_bytes=60 * 2**20
        ),
        cost_estimate=pl.CostEstimate(
            flops=12 * pairs * feat * ff, bytes_accessed=8 * feat * ff, transcendentals=pairs * ff
        ),
        name="moe_layer",
    )(tokens, gates.T, expert_ids.T, d_mixed, w_up, w_down)


def solution(mesh):
    in_specs = (
        P("expert", "dp"),
        P("expert", None),
        P("expert", None),
        P("expert", "dp"),
        P("expert", "dp", None),
        P("expert", None, "dp"),
    )
    out_specs = (
        P("expert", "dp"),
        P("expert", "dp"),
        P("expert", "dp", None),
        P("expert", None, "dp"),
    )
    return jax.shard_map(
        per_device, mesh=mesh, in_specs=in_specs, out_specs=out_specs, check_vma=False
    )
```

```python
import functools

import jax
import jax.numpy as jnp
from jax import lax
from jax.experimental import pallas as pl
from jax.experimental.pallas import tpu as pltpu
from jax.sharding import PartitionSpec as P

MESH = pl.DeviceIdType.MESH
F32 = jnp.float32
BF16 = jnp.bfloat16


def tiles(extent, size, body):
    size = min(size, extent)

    def step(j, carry):
        body(pl.multiple_of(j * size, size), size)
        return carry

    lax.fori_loop(0, extent // size, step, 0)


def flip(value, mask, limit):
    result = value
    bit = 1
    while bit < limit:
        on = (mask // bit) % 2
        result = result + bit * on * (1 - 2 * ((value // bit) % 2))
        bit *= 2
    return result


def differ(a, b, limit):
    result = 0
    bit = 1
    while bit < limit:
        result = result + bit * ((a // bit + b // bit) % 2)
        bit *= 2
    return result


def mm(a, b, da, db):
    return lax.dot_general(a, b, (((da,), (db,)), ((), ())), preferred_element_type=F32)


def kernel(
    cfg,
    tok, gates, ids, dmix, w_up, w_down,
    both, grad_up, grad_down,
    gt, sx, rows, wu, wd, part, rsbuf, hid, pre, own, cx, cy, cz, mt, mx,
    zs, zr, mzs, mzr, ys, yr, mys, myr, xs, xr, mxs, mxr,
    rss, rsr, ags, agr, cxs, cxr, cys, cyr, czs, czr, loc,
):
    groups, nd, t_rows, top, feat, ff, cap = cfg
    planes = groups // 4
    count = 2 * planes
    half = 2 * cap
    chunk = 4 * cap
    share = chunk // nd
    e = lax.axis_index("expert")
    me = lax.axis_index("dp")
    z, y, x = e // 4, (e // 2) % 2, e % 2
    e_x = e + 1 - 2 * x
    e_y = e + 2 - 4 * y

    def ring_of(i):
        kind, m = i // planes, i % planes
        r = (m + kind) % planes
        if planes == 4:
            r = m + kind * (2 - 2 * m + (m // 2) * (3 - 2 * (m % 2)))
            inner = (z % 3 + 2) // 3
            r = r + inner * (r // 2) * (5 - 2 * r)
        return r

    def slot_of(i):
        return (i // planes) * planes + ring_of(i)

    def z_peer(r):
        return flip(z, r, planes) * 4 + y * 2 + x

    def send(src, dst, ssem, rsem, expert=None, dp=None):
        where = {"expert": expert} if dp is None else {"dp": dp}
        return pltpu.make_async_remote_copy(
            src_ref=src, dst_ref=dst, send_sem=ssem, recv_sem=rsem,
            device_id=where, device_id_type=MESH,
        )

    def z_next(s, origin, way):
        there = z + 1 - 2 * way
        return there * 4 + y * 2 + x, (s // planes) * planes + differ(origin, there, planes)

    def z_copy(s, origin, way, src=None):
        peer, slot = z_next(s, origin, way)
        src = gt.at[s, 0] if src is None else src
        return send(src, gt.at[slot, 0], zs.at[s, way], zr.at[slot], peer)

    def mz_copy(s, origin, way):
        peer, slot = z_next(s, origin, way)
        return send(mt.at[s, 0], mt.at[slot, 0], mzs.at[s, way], mzr.at[slot], peer)

    def onward(s, act):
        origin = flip(z, s % planes, planes)

        @pl.when(jnp.logical_and(origin < z, z < planes - 1))
        def _():
            act(origin, 0)

        @pl.when(jnp.logical_and(origin > z, z > 0))
        def _():
            act(origin, 1)

    def outward(act):
        @pl.when(z < planes - 1)
        def _():
            act(z, 0)

        @pl.when(z > 0)
        def _():
            act(z, 1)

    def y_copy(i):
        return send(gt.at[i, 0], gt.at[i, 1], ys.at[i], yr.at[i], e_y)

    def my_copy(i):
        return send(mt.at[i, 0], mt.at[i, 1], mys.at[i], myr.at[i], e_y)

    def x_copy(i, yy):
        return send(
            sx.at[i, pl.ds(yy * cap, cap)], rows.at[i, pl.ds(half + yy * cap, cap)],
            xs.at[i, yy], xr.at[i, yy], e_x,
        )

    def mx_copy(i, yy):
        return send(mt.at[i, yy], mx.at[i, yy], mxs.at[i, yy], mxr.at[i, yy], e_x)

    def rs_copy(i, h, o):
        peer = (me + o) % nd
        return send(
            part.at[h, pl.ds(pl.multiple_of(peer * share, share), share)],
            rsbuf.at[i, o - 1], rss.at[i, o - 1], rsr.at[i, o - 1], dp=peer,
        )

    def ag_copy(i, o):
        mine = hid.at[i, pl.ds(pl.multiple_of(me * share, share), share)]
        return send(mine, mine, ags.at[i, o - 1], agr.at[i, o - 1], dp=(me + o) % nd)

    def cx_copy(i, yy):
        here = pl.ds(yy * cap, cap)
        return send(sx.at[i, here], cx.at[i, here], cxs.at[i, yy], cxr.at[i, yy], e_x)

    def cy_copy(i):
        return send(gt.at[i, 1], cy.at[i], cys.at[i], cyr.at[i], e_y)

    def cz_copy(i):
        return send(gt.at[i, 0], cz.at[i], czs.at[i], czr.at[i], z_peer(i % planes))

    tok_in = pltpu.make_async_copy(tok, gt.at[0, 0], loc.at[0])
    dmix_in = pltpu.make_async_copy(dmix, gt.at[planes, 0], loc.at[1])
    wu_in = pltpu.make_async_copy(w_up.at[0], wu, loc.at[2])
    wd_in = pltpu.make_async_copy(w_down.at[0], wd, loc.at[3])
    tok_in.start()
    dmix_in.start()
    wu_in.start()
    wd_in.start()

    barrier = pltpu.get_barrier_semaphore()
    peers = [{"expert": z_peer(r)} for r in range(1, planes)]
    peers += [{"expert": e_x}, {"expert": e_y}]
    peers += [{"dp": (me + o) % nd} for o in range(1, nd)]
    for peer in peers:
        pl.semaphore_signal(barrier, inc=1, device_id=peer, device_id_type=MESH)
    pl.semaphore_wait(barrier, len(peers))

    outward(lambda origin, way: z_copy(0, origin, way, tok).start())

    tok_in.wait()
    y_copy(0).start()

    expert_row = lax.broadcasted_iota(jnp.int32, (groups, t_rows), 0)
    chosen = jnp.zeros((groups, t_rows), F32)
    weight = jnp.zeros((groups, t_rows), F32)
    for k in range(top):
        hit = ids[k : k + 1, :] == expert_row
        chosen = chosen + jnp.where(hit, 1.0, 0.0)
        weight = weight + jnp.where(hit, gates[k : k + 1, :], 0.0)
    lane = lax.broadcasted_iota(jnp.int32, (t_rows, t_rows), 1)
    row = lax.broadcasted_iota(jnp.int32, (t_rows, t_rows), 0)
    before = jnp.where(row < lane, 1.0, 0.0).astype(BF16)
    place = mm(chosen.astype(BF16), before, 1, 0)
    mt[0, 0, :groups, :] = jnp.where(chosen > 0.0, place, -1.0)
    mt[0, 0, groups:, :] = weight
    outward(lambda origin, way: mz_copy(0, origin, way).start())

    slot = lax.broadcasted_iota(jnp.int32, (cap, t_rows), 0).astype(F32)

    def pick(table, expert):
        hot = slot == table[pl.ds(expert, 1), :]
        gate = jnp.sum(jnp.where(hot, table[pl.ds(groups + expert, 1), :], 0.0), 1, keepdims=True)
        return jnp.where(hot, 1.0, 0.0).astype(BF16), gate

    def select(i, yy):
        r = i % planes
        hot_n, gate_n = pick(mt.at[r, yy], e_x)
        hot_o, gate_o = pick(mt.at[r, yy], e)
        hot = jnp.concatenate([hot_n, hot_o], 0)
        gate = jnp.concatenate([gate_n, gate_o], 0)
        gate = jnp.where(i < planes, 1.0, gate)

        def tile(at, size):
            got = mm(hot, gt[i, yy, :, pl.ds(at, size)], 1, 0) * gate
            got = got.astype(BF16)
            sx[i, yy * cap : (yy + 1) * cap, pl.ds(at, size)] = got[:cap]
            rows[i, yy * cap : (yy + 1) * cap, pl.ds(at, size)] = got[cap:]

        tiles(feat, 512, tile)
        x_copy(i, yy).start()

        @pl.when(i < planes)
        def _():
            mx_copy(i, yy).start()

    def stage_z(i, order):
        @pl.when(i == planes)
        def _():
            dmix_in.wait()

        @pl.when(i % planes != 0)
        def _():
            send(gt.at[i, 0], gt.at[i, 0], zs.at[i, 0], zr.at[i], e_x).wait_recv()
            onward(i, lambda origin, way: z_copy(i, origin, way).start())

            @pl.when(i < planes)
            def _():
                send(mt.at[i, 0], mt.at[i, 0], mzs.at[i, 0], mzr.at[i], e_x).wait_recv()
                onward(i, lambda origin, way: mz_copy(i, origin, way).start())

        @pl.when(i != 0)
        def _():
            y_copy(i).start()

        @pl.when(i < planes)
        def _():
            my_copy(i).start()

        @pl.when(order == planes - 1)
        def _():
            outward(lambda origin, way: z_copy(planes, origin, way, dmix).start())

    def stage_y(i):
        y_copy(i).wait()

        @pl.when(i < planes)
        def _():
            my_copy(i).wait()

        select(i, 1)

    def stage_in(i, h):
        for yy in range(2):
            x_copy(i, yy).wait()

        @pl.when(i < planes)
        def _():
            for yy in range(2):
                mx_copy(i, yy).wait()

            @pl.when(i == 0)
            def _():
                wu_in.wait()

            def tile(at, size):
                part[h, :, pl.ds(at, size)] = mm(
                    rows[i], wu[:, pl.ds(at, size)], 1, 0
                ).astype(BF16)

            tiles(ff, 256, tile)

        @pl.when(i >= planes)
        def _():
            def tile(at, size):
                part[h, :, pl.ds(at, size)] = mm(
                    rows[i], wd[pl.ds(at, size), :], 1, 1
                ).astype(BF16)

            tiles(ff, 256, tile)

        for o in range(1, nd):
            rs_copy(i, h, o).start()

    def stage_act(i, h):
        for o in range(1, nd):
            rs_copy(i, h, o).wait()
        r = i % planes
        base = me * share

        def tile(at, size):
            here = pl.ds(pl.multiple_of(base + at, size), size)
            total = part[h, here, :].astype(F32)
            for o in range(1, nd):
                total = total + rsbuf[i, o - 1, pl.ds(at, size), :].astype(F32)

            @pl.when(i < planes)
            def _():
                pre[r, pl.ds(at, size), :] = total
                hid[i, here, :] = (total / (1.0 + jnp.exp(-total))).astype(BF16)

            @pl.when(i >= planes)
            def _():
                value = pre[r, pl.ds(at, size), :]
                s = 1.0 / (1.0 + jnp.exp(-value))
                hid[i, here, :] = (total * s * (1.0 + value * (1.0 - s))).astype(BF16)

        tiles(share, 16, tile)
        for o in range(1, nd):
            ag_copy(i, o).start()

    def stage_out(i, h):
        for o in range(1, nd):
            ag_copy(i, o).wait()

        def store(at, size, got):
            got = got.astype(BF16)
            own[h, :, pl.ds(at, size)] = got[:half]
            sx[i, :, pl.ds(at, size)] = got[half:]

        @pl.when(i < planes)
        def _():
            @pl.when(i == 0)
            def _():
                wd_in.wait()

            gate = jnp.concatenate(
                [pick(t.at[i, yy], e)[1] for t in (mt, mx) for yy in range(2)], 0
            )

            def tile(at, size):
                store(at, size, mm(hid[i], wd[:, pl.ds(at, size)], 1, 0) * gate)

            tiles(feat, 256, tile)

        @pl.when(i >= planes)
        def _():
            def tile(at, size):
                store(at, size, mm(hid[i], wu[pl.ds(at, size), :], 1, 1))

            tiles(feat, 256, tile)

        cx_copy(i, 1).start()
        cx_copy(i, 0).start()

    def placed(i, h, yy):
        r = i % planes
        hot = jnp.concatenate([pick(mt.at[r, yy], e)[0], pick(mt.at[r, yy], e_x)[0]], 0)
        there = slice(yy * cap, (yy + 1) * cap)

        def tile(at, size):
            data = jnp.concatenate(
                [own[h, there, pl.ds(at, size)], cx[i, there, pl.ds(at, size)]], 0
            )
            return mm(hot, data, 0, 0)

        return tile

    def stage_cx(i, h):
        cx_copy(i, 1).wait()
        sums = placed(i, h, 1)

        def tile(at, size):
            gt[i, 1, :, pl.ds(at, size)] = sums(at, size).astype(BF16)

        tiles(feat, 512, tile)
        cy_copy(i).start()

    def stage_cy(i, h):
        cx_copy(i, 0).wait()
        cy_copy(i).wait()

        @pl.when(i % planes != 0)
        def _():
            onward(i, lambda origin, way: z_copy(i, origin, way).wait_send())

        sums = placed(i, h, 0)

        def tile(at, size):
            here = pl.ds(at, size)
            gt[i, 0, :, here] = (sums(at, size) + cy[i, :, here].astype(F32)).astype(BF16)

        tiles(feat, 512, tile)

        @pl.when(i % planes != 0)
        def _():
            cz_copy(i).start()

    def finish_tokens():
        for i in range(1, planes):
            cz_copy(i).wait()

        def tile(at, size):
            here = pl.ds(at, size)
            total = gt[0, 0, here, :].astype(F32)
            for i in range(1, planes):
                total = total + cz[i, here, :].astype(F32)
            both[0, here, :] = total.astype(BF16)

        tiles(t_rows, 16, tile)

    def live(i, body):
        @pl.when(jnp.logical_and(i >= 0, i < count))
        def _():
            body(slot_of(i), i % 2)

    def tick(i, carry):
        live(i - 4, stage_act)
        live(i - 6, stage_cy)
        live(i - 5, stage_cx)
        live(i - 4, stage_out)
        live(i, lambda s, h: stage_z(s, i))
        live(i, lambda s, h: select(s, 0))
        live(i - 2, lambda s, h: stage_y(s))
        live(i - 3, stage_in)
        return carry

    lax.fori_loop(0, count + 4, tick, 0)

    pairs = [(i, i + planes) for i in range(planes)]

    def down_tile(at, size):
        total = None
        for a, b in pairs:
            term = mm(hid[a, :, pl.ds(at, size)], rows[b], 0, 0)
            total = term if total is None else total + term
        wd[pl.ds(at, size), :] = total.astype(BF16)

    tiles(ff, 256, down_tile)
    down_out = pltpu.make_async_copy(wd, grad_down.at[0], loc.at[3])
    down_out.start()

    stage_cy(slot_of(count - 2), count % 2)
    stage_cx(slot_of(count - 1), (count - 1) % 2)

    def up_tile(at, size):
        total = None
        for a, b in pairs:
            term = mm(rows[a, :, pl.ds(at, size)], hid[b], 0, 0)
            total = term if total is None else total + term
        wu[pl.ds(at, size), :] = total.astype(BF16)

    tiles(feat, 512, up_tile)
    up_out = pltpu.make_async_copy(wu, grad_up.at[0], loc.at[2])
    up_out.start()

    finish_tokens()

    cx_copy(planes, 0).wait()
    cy_copy(planes).wait()
    for s in range(planes + 1, count):
        cz_copy(s).wait()
    sums = placed(planes, (count - 1) % 2, 0)

    def last_tile(at, size):
        here = pl.ds(at, size)
        total = sums(at, size) + cy[planes, :, here].astype(F32)
        for s in range(planes + 1, count):
            total = total + cz[s, :, here].astype(F32)
        both[1, :, here] = total.astype(BF16)

    tiles(feat, 512, last_tile)
    outward(lambda origin, way: z_copy(0, origin, way, tok).wait_send())
    outward(lambda origin, way: z_copy(planes, origin, way, dmix).wait_send())
    outward(lambda origin, way: mz_copy(0, origin, way).wait_send())
    for i in range(1, planes):
        onward(i, lambda origin, way, i=i: mz_copy(i, origin, way).wait_send())
    down_out.wait()
    up_out.wait()


def per_device(tokens, gates, expert_ids, d_mixed, w_up, w_down):
    t_rows, feat = tokens.shape
    top = expert_ids.shape[1]
    ff = w_up.shape[2]
    groups = lax.axis_size("expert")
    nd = lax.axis_size("dp")
    hot_rows = t_rows // 2
    cold_rows = (t_rows * top - hot_rows + groups - 2) // (groups - 1)
    cap = max(hot_rows, cold_rows)
    planes = groups // 4
    count = 2 * planes
    half, chunk = 2 * cap, 4 * cap
    share = chunk // nd
    cfg = (groups, nd, t_rows, top, feat, ff, cap)
    dma = pltpu.SemaphoreType.DMA
    vm = pltpu.VMEM
    scratch = [
        vm((count, 2, t_rows, feat), BF16),
        vm((count, half, feat), BF16),
        vm((count, chunk, feat), BF16),
        vm((feat, ff), BF16),
        vm((ff, feat), BF16),
        vm((2, chunk, ff), BF16),
        vm((count, nd - 1, share, ff), BF16),
        vm((count, chunk, ff), BF16),
        vm((planes, share, ff), F32),
        vm((2, half, feat), BF16),
        vm((count, half, feat), BF16),
        vm((count, t_rows, feat), BF16),
        vm((count, t_rows, feat), BF16),
        vm((planes, 2, 2 * groups, t_rows), F32),
        vm((planes, 2, 2 * groups, t_rows), F32),
    ]
    for shape in (
        [(count, 2), (count,), (planes, 2), (planes,)] + [(count,)] * 2 + [(planes,)] * 2
        + [(count, 2)] * 2 + [(planes, 2)] * 2 + [(count, nd - 1)] * 4 + [(count, 2)] * 2 + [(count,)] * 4 + [(4,)]
    ):
        scratch.append(dma(shape))
    pairs = groups * cap
    space = pl.BlockSpec(memory_space=pl.ANY)
    vmem = pl.BlockSpec(memory_space=pltpu.VMEM)
    both, grad_up, grad_down = pl.pallas_call(
        functools.partial(kernel, cfg),
        out_shape=(
            jax.ShapeDtypeStruct((2, t_rows, feat), BF16),
            jax.ShapeDtypeStruct(w_up.shape, BF16),
            jax.ShapeDtypeStruct(w_down.shape, BF16),
        ),
        in_specs=[space, vmem, vmem, space, space, space],
        out_specs=(vmem, space, space),
        scratch_shapes=scratch,
        compiler_params=pltpu.CompilerParams(
            collective_id=0, has_side_effects=True, vmem_limit_bytes=60 * 2**20
        ),
        cost_estimate=pl.CostEstimate(
            flops=12 * pairs * feat * ff, bytes_accessed=8 * feat * ff, transcendentals=pairs * ff
        ),
        name="moe_layer",
    )(tokens, gates.T, expert_ids.T, d_mixed, w_up, w_down)
    return both[0], both[1], grad_up, grad_down


def solution(mesh):
    in_specs = (
        P("expert", "dp"),
        P("expert", None),
        P("expert", None),
        P("expert", "dp"),
        P("expert", "dp", None),
        P("expert", None, "dp"),
    )
    out_specs = (
        P("expert", "dp"),
        P("expert", "dp"),
        P("expert", "dp", None),
        P("expert", None, "dp"),
    )
    return jax.shard_map(
        per_device, mesh=mesh, in_specs=in_specs, out_specs=out_specs, check_vma=False
    )
```
